256 devices in a mesh: grp: 4 (over y_lo, core), dom: 64 (over x, y_hi, z).
Axes of the slice: x: 4, y: 4 (y_hi: 2, y_lo: 2; y = y_hi * 2 + y_lo), z: 8, core: 2. Of those that a mesh axis runs over, the one named last changes fastest.
Arguments:
- left_table: float32 [262144, 256], P(('grp', 'dom')), may hold values from -1.5 to 1.5
- left_state: float32 [262144], P(('grp', 'dom')), may hold values from 0.001 to 0.1
- right_table: float32 [262144, 256], P(('grp', 'dom')), may hold values from -1.5 to 1.5
- right_state: float32 [262144], P(('grp', 'dom')), may hold values from 0.001 to 0.1
- operators: float32 [2304, 256], P(('grp', 'dom')), may hold values from 0.1 to 1.9
- operator_state: float32 [2304, 256], P(('grp', 'dom')), may hold values from 0.01 to 1
- heads: int32 [2, 1048576], P(None, ('grp', 'dom')), may hold values from 0 to 1023
- tails: int32 [2, 1048576], P(None, ('grp', 'dom')), may hold values from 0 to 1023
- relations: int32 [2, 1048576], P(None, ('grp', 'dom')), may hold values from 0 to 2303
- negatives: int32 [2, 2048, 512], P(None, ('grp', 'dom')), may hold values from 0 to 1023
- edge_counts: int32 [2, 256], P(None, ('grp', 'dom')), may hold values from 1 to 4096, 524288 in all within a row
- partner_mask: int32 [1], replicated, may hold values from 1 to 63
Outputs:
- new_left_table: float32 [262144, 256], P(('grp', 'dom'))
- new_left_state: float32 [262144], P(('grp', 'dom'))
- new_right_table: float32 [262144, 256], P(('grp', 'dom'))
- new_right_state: float32 [262144], P(('grp', 'dom'))
- new_operators: float32 [2304, 256], P(('grp', 'dom'))
The draws below stay inside these ranges and needn't reach their ends.
Inputs may be any that keep to these rules, and one draw needn't show every extreme that they name: `edge_counts`: in each round some bucket has exactly 4096 live edges.
All inputs are finite; a program needn't handle non-finite values. No bound on the sum of `edge_counts` on one device may be relied on, other than what follows from the above.
Results may differ from the reference program's by a relative error of at most 0.0003.
Values sent between devices are 32-bit elements; how exact they have to be, the bound alone decides.
No kernel may reach another device: no remote copies, remote signals or barrier semaphores. Data moves between devices by JAX's collectives and lax.ppermute only.
A program may use at most 64 MiB of HBM per device.

```python
import math
import jax
import jax.numpy as jnp
import numpy as np
from jax import lax

D = 256
REL = 2304
P_SIZE = 1024
SPAN = 512
NEG = 512
SPANS = 8
ROUNDS = 2
E_CAP = 4096
BUCKETS = 256
N_GRP = 4
N_DOM = 64


def with_ends(result, stream_key, least, top_value):
    longest = result.shape.index(max(result.shape))
    spots = []
    for shift in (0, 1):
        where = [jax.random.randint(jax.random.fold_in(stream_key, axis), (), 0, length) for axis, length in enumerate(result.shape)]
        where[longest] = (where[longest] + shift) % result.shape[longest]
        spots.append(tuple(where))
    return result.at[spots[0]].set(least).at[spots[1]].set(top_value)


def level_of(own_key, extent, cuts, smallest, high):
    factor_of, own = 1.0, jax.random.fold_in(own_key, 6)
    for position, shards_of in cuts:
        steps = jnp.exp(jax.random.uniform(jax.random.fold_in(own, position), (shards_of,), jnp.float32, smallest / len(cuts), high / len(cuts)))
        factor_of = factor_of * jnp.repeat(steps, extent[position] // shards_of).reshape([-1 if axis == position else 1 for axis in range(len(extent))])
    return factor_of


def cumulative_ranks(count, lean):
    portions = [(1 << 20) // math.isqrt(grade ** lean) + 1 for grade in range(1, count + 1)]
    width = 1 + sum(portions) // (1 << 30)
    return np.cumsum(np.array([max(1, weight // width) for weight in portions]))


def skewed_ids(own_key, extent, count, slope):
    listing = cumulative_ranks(count, slope)
    lot = jax.random.randint(jax.random.fold_in(own_key, 1), extent, 0, int(listing[count - 1]))
    standing = jnp.searchsorted(jnp.asarray(listing, jnp.int32), lot, side="right")
    return jax.random.permutation(jax.random.fold_in(own_key, 2), count)[standing].astype(jnp.int32)


def profile(amount, total, bound, skew):
    loads = [(1 << 20) // math.isqrt(rank ** skew) + 1 for rank in range(2, amount + 1)]
    rest, counts = total - bound - (amount - 1), [1] * (amount - 1)
    while rest > 0:
        free = [i for i in range(amount - 1) if counts[i] < bound]
        mass, remaining = sum([loads[i] for i in free]), rest
        for i in free:
            addition = min(bound - counts[i], max(1, remaining * loads[i] // mass), rest)
            counts[i] = counts[i] + addition
            rest = rest - addition
    return np.array([bound] + counts)


def ragged_sizes(key, count, total, limit, skew):
    if count == 2:
        one = jax.random.randint(key, (), max(1, total - limit), min(limit, total - 1) + 1)
        return jnp.stack([one, total - one])
    lengths = jnp.asarray(profile(count, total, limit, skew), jnp.int32)
    couples = (count - 1) // 2
    source_of, taker = lengths[1:1 + 2 * couples:2], lengths[2:2 + 2 * couples:2]
    margin = jnp.minimum(source_of - 1, limit - taker)
    passed = jax.random.randint(jax.random.fold_in(key, 1), (couples,), 0, 1 << 20) % (margin + 1)
    lengths = lengths.at[1:1 + 2 * couples:2].set(source_of - passed).at[2:2 + 2 * couples:2].set(taker + passed)
    return lengths[jax.random.permutation(jax.random.fold_in(key, 2), count)]


def bell_draw(key, shape, scale, most, split=(), held_as=jnp.bfloat16):
    result = jax.random.normal(key, shape, jnp.float32) * scale
    if len(split) > 0:
        result = level_of(key, shape, split, -0.22, 0.18) * result
    return jnp.clip(result, min=-most, max=most).astype(held_as)


def setup_inputs(seed: int = 0) -> dict:
    arg_keys = jax.random.split(jax.random.key(seed), 13)
    left_table = bell_draw(arg_keys[0], (BUCKETS * P_SIZE, D), 0.25, 1.5, ((0, 256),), jnp.float32)
    left_state = jnp.clip(jnp.exp(math.log(0.1) - 4.6051702 * jax.random.uniform(arg_keys[1], (BUCKETS * P_SIZE,), jnp.float32) ** level_of(arg_keys[1], (BUCKETS * P_SIZE,), ((0, 256),), -0.2, 0.2)), 0.001, 0.1)
    right_table = bell_draw(arg_keys[2], (BUCKETS * P_SIZE, D), 0.25, 1.5, ((0, 256),), jnp.float32)
    right_state = jnp.clip(jnp.exp(math.log(0.1) - 4.6051702 * jax.random.uniform(arg_keys[3], (BUCKETS * P_SIZE,), jnp.float32) ** level_of(arg_keys[3], (BUCKETS * P_SIZE,), ((0, 256),), -0.2, 0.2)), 0.001, 0.1)
    operators = jnp.clip(1.0 + 0.18 * jax.random.normal(arg_keys[4], (REL, D), jnp.float32), 0.1, 1.9)
    operator_state = jnp.clip(jnp.exp(math.log(1.0) - 4.6051702 * jax.random.uniform(arg_keys[5], (REL, D), jnp.float32) ** level_of(arg_keys[5], (REL, D), ((0, 256),), -0.2, 0.2)), 0.01, 1.0)
    heads = with_ends(skewed_ids(arg_keys[6], (ROUNDS, BUCKETS * E_CAP), P_SIZE, 1), jax.random.fold_in(arg_keys[6], 3), 0, P_SIZE - 1).astype(jnp.int32)
    tails = with_ends(skewed_ids(arg_keys[7], (ROUNDS, BUCKETS * E_CAP), P_SIZE, 1), jax.random.fold_in(arg_keys[7], 3), 0, P_SIZE - 1).astype(jnp.int32)
    relations = with_ends(jax.random.randint(arg_keys[8], (ROUNDS, BUCKETS * E_CAP), 0, REL), jax.random.fold_in(arg_keys[8], 1), 0, REL - 1).astype(jnp.int32)
    negatives = with_ends(jax.random.randint(arg_keys[9], (ROUNDS, BUCKETS * SPANS, NEG), 0, P_SIZE), jax.random.fold_in(arg_keys[9], 1), 0, P_SIZE - 1).astype(jnp.int32)
    edge_counts = jax.vmap(lambda own: ragged_sizes(own, BUCKETS, BUCKETS * E_CAP // 2, E_CAP, 2))(jax.random.split(arg_keys[10], ROUNDS)).reshape((ROUNDS, BUCKETS)).astype(jnp.int32)
    partner_mask = jax.random.randint(arg_keys[11], (1,), 1, N_DOM).astype(jnp.int32)
    return dict(left_table=left_table, left_state=left_state, right_table=right_table, right_state=right_state, operators=operators, operator_state=operator_state, heads=heads, tails=tails, relations=relations, negatives=negatives, edge_counts=edge_counts, partner_mask=partner_mask)


embed_rate = 0.1
operator_rate = 0.5
highest = lax.Precision.HIGHEST

def block_update(carried, head_index, tail_index, rel_index, neg_index, edge_mask, operator_rows):
    left_part, left_acc, right_part, right_acc, rel_grads = carried
    head_rows = left_part[head_index]
    tail_rows = right_part[tail_index]
    neg_rows = right_part[neg_index]
    diag_rows = operator_rows[rel_index]
    scaled_heads = head_rows * diag_rows
    positive = lax.optimization_barrier(jnp.sum(scaled_heads * tail_rows, axis=1))
    negative = jnp.einsum('cd,nd->cn', scaled_heads, neg_rows, precision=highest)
    pos_grad = -jax.nn.sigmoid(-positive) * edge_mask
    neg_grad = jax.nn.sigmoid(negative) * (edge_mask / NEG)[:, None]
    head_side = pos_grad[:, None] * tail_rows + jnp.dot(neg_grad, neg_rows, precision=highest)
    tail_side = pos_grad[:, None] * scaled_heads
    neg_side = jnp.einsum('cn,cd->nd', neg_grad, scaled_heads, precision=highest)
    left_grad = jnp.zeros_like(left_part).at[head_index].add(head_side * diag_rows)
    right_grad = jnp.zeros_like(right_part).at[tail_index].add(tail_side).at[neg_index].add(neg_side)
    rel_grads = rel_grads.at[rel_index].add(head_side * head_rows)
    left_acc = left_acc + lax.optimization_barrier(jnp.mean(left_grad * left_grad, axis=1))
    left_part = left_part - embed_rate * left_grad / jnp.sqrt(left_acc)[:, None]
    right_acc = right_acc + lax.optimization_barrier(jnp.mean(right_grad * right_grad, axis=1))
    right_part = right_part - embed_rate * right_grad / jnp.sqrt(right_acc)[:, None]
    return (left_part, left_acc, right_part, right_acc, rel_grads)

def train_reference(carried, head_list, tail_list, rel_list, neg_list, edge_count, operator_rows):
    for block_index in range(SPANS):
        start = block_index * SPAN
        positions = start + jnp.arange(SPAN, dtype=jnp.int32)
        edge_mask = (positions < edge_count).astype(carried[0].dtype)
        carried = block_update(carried, head_list[start:start + SPAN], tail_list[start:start + SPAN], rel_list[start:start + SPAN], neg_list[block_index], edge_mask, operator_rows)
    return carried

def reference(left_table, left_state, right_table, right_state, operators, operator_state, heads, tails, relations, negatives, edge_counts, partner_mask):
    devices = N_GRP * N_DOM
    tables = (left_table.reshape(devices, P_SIZE, D), left_state.reshape(devices, P_SIZE), right_table.reshape(devices, P_SIZE, D), right_state.reshape(devices, P_SIZE))
    head_all = heads.reshape(ROUNDS, devices, E_CAP)
    tail_all = tails.reshape(ROUNDS, devices, E_CAP)
    rel_all = relations.reshape(ROUNDS, devices, E_CAP)
    neg_all = negatives.reshape(ROUNDS, devices, SPANS, NEG)

    def run_round(round_index, tables, rel_grads):

        def visit(grads, inputs):
            outcome = train_reference(inputs[:4] + (grads,), inputs[4], inputs[5], inputs[6], inputs[7], inputs[8], operators)
            return (outcome[4], outcome[:4])
        inputs = tables + (head_all[round_index], tail_all[round_index], rel_all[round_index], neg_all[round_index], edge_counts[round_index])
        rel_grads, tables = lax.scan(visit, rel_grads, inputs)
        return (tables, rel_grads)
    rel_grads = jnp.zeros((REL, D), jnp.float32)
    tables, rel_grads = run_round(0, tables, rel_grads)
    index = jnp.arange(devices, dtype=jnp.int32)
    partner = index // N_DOM * N_DOM + jnp.bitwise_xor(index % N_DOM, partner_mask[0])
    tables = (tables[0], tables[1], tables[2][partner], tables[3][partner])
    tables, rel_grads = run_round(1, tables, rel_grads)
    new_acc = operator_state + rel_grads * rel_grads
    new_operators = operators - operator_rate * rel_grads / jnp.sqrt(new_acc)
    return (tables[0].reshape(devices * P_SIZE, D), tables[1].reshape(devices * P_SIZE), tables[2].reshape(devices * P_SIZE, D), tables[3].reshape(devices * P_SIZE), new_operators)
```

```python
import jax
import jax.numpy as jnp
from jax import lax
from jax.experimental import pallas as pl
from jax.experimental.pallas import tpu as pltpu
from jax.sharding import PartitionSpec as P

D = 256
PART = 1024
SPAN = 512
REL = 2304
VMEM = pl.BlockSpec(memory_space=pltpu.VMEM)
SMEM = pl.BlockSpec(memory_space=pltpu.SMEM)
AXES = ("grp", "dom")
STAGES = ((1, 2, 3, 4, 5, 6, 7), (16, 32, 48), (8, 128, 136), (64,))


def split(x):
    high = x.astype(jnp.bfloat16)
    return high, (x - high.astype(jnp.float32)).astype(jnp.bfloat16)


def mm(x, y):
    return jnp.dot(x, y, preferred_element_type=jnp.float32)


def mm_nt(x, y):
    return lax.dot_general(x, y, (((1,), (1,)), ((), ())), preferred_element_type=jnp.float32)


def block_turns(count_ref):
    return (count_ref[0] + SPAN - 1) // SPAN


def one_hot(rows, index_row, base=0):
    ids = base + lax.broadcasted_iota(jnp.int32, (rows, SPAN), 0)
    return jnp.where(ids == index_row, 1.0, 0.0).astype(jnp.bfloat16)


def gather_kernel(count_ref, rel_ref, ops_ref, w_ref, hot, ops_split):
    ops_t = ops_ref[...].T
    high, low = split(ops_t)
    ops_split[0:D] = high
    ops_split[D : 2 * D] = low

    def one(k, _):
        index_row = rel_ref[pl.ds(k, 1), :]
        for c in range(REL // 256):
            hot[c * 256 : (c + 1) * 256] = one_hot(256, index_row, c * 256)
        both = mm(ops_split[...], hot[...])
        w_ref[k] = both[:D] + both[D:]
        return 0

    lax.fori_loop(0, block_turns(count_ref), one, 0)


def grads_kernel(count1_ref, count2_ref, rel1_ref, rel2_ref, z1_ref, z2_ref, g_ref, hot, acc):
    acc[...] = jnp.zeros_like(acc)

    def scatter(rel_ref, z_ref, turns):
        def one(k, _):
            index_row = rel_ref[pl.ds(k, 1), :]
            for c in range(REL // 256):
                rows = slice(c * 256, (c + 1) * 256)
                hot[rows] = one_hot(256, index_row, c * 256)
            acc[...] += mm_nt(hot[...], z_ref[k])
            return 0

        lax.fori_loop(0, turns, one, 0)

    scatter(rel1_ref, z1_ref, block_turns(count1_ref))
    scatter(rel2_ref, z2_ref, block_turns(count2_ref))
    g_ref[...] = acc[:, :D] + acc[:, D:]


def train_kernel(second, count_ref, heads_ref, tails_ref, negs_ref, w_ref, l_ref, ls_ref, r_ref, rs_ref,
                 l_out, ls_out, r_out, rs_out, z_ref,
                 lt, rt, l_split, r_split, r_cols, hot, s3, cat, score, c_high, c_low):
    def set_left(value):
        lt[...] = value
        high, low = split(value)
        l_split[0:D] = high
        l_split[D : 2 * D] = low

    def set_right(value):
        rt[...] = value
        high, low = split(value)
        r_split[0:D] = high
        r_split[D : 2 * D] = low
        across = value.T
        high, low = split(across)
        r_cols[:, 0:D] = high
        r_cols[:, D : 2 * D] = high
        r_cols[:, 2 * D : 3 * D] = low

    if second:
        set_left(l_ref[...])
        set_right(r_ref[0:D, :])
        rs_out[...] = r_ref[D : D + 1, :]
    else:
        set_left(l_ref[...].T)
        set_right(r_ref[...].T)
        rs_out[...] = rs_ref[...]
    ls_out[...] = ls_ref[...]
    count = count_ref[0]

    def one(k, _):
        head_row = heads_ref[pl.ds(k, 1), :]
        tail_row = tails_ref[pl.ds(k, 1), :]
        neg_row = negs_ref[pl.ds(k, 1), :]
        slots = k * SPAN + lax.broadcasted_iota(jnp.int32, (1, SPAN), 1)
        live = jnp.where(slots < count, 1.0, 0.0)
        half = live * (0.5 / SPAN)
        for c in range(8):
            hot[c * 128 : (c + 1) * 128] = one_hot(128, head_row, c * 128)
        w_t = w_ref[k]
        both = mm(l_split[...], hot[...])
        h_t = both[:D] + both[D:]
        s_high, s_low = split(h_t * w_t)
        s3[0:D] = s_high
        s3[D : 2 * D] = s_low
        s3[2 * D : 3 * D] = s_high
        score[...] = mm(r_cols[...], s3[...])
        positive = jnp.zeros((8, SPAN), jnp.float32)
        for c in range(PART // 32):
            rows = slice(c * 32, (c + 1) * 32)
            ids = c * 32 + lax.broadcasted_iota(jnp.int32, (32, SPAN), 0)
            a = score[rows]
            times = jnp.sum(jnp.where(ids == neg_row, 1.0, 0.0), axis=1, keepdims=True)
            picked = jnp.where(ids == tail_row, a, 0.0)
            positive = positive + (picked[0:8] + picked[8:16]) + (picked[16:24] + picked[24:32])
            score[rows] = (jnp.tanh(0.5 * a) + 1.0) * times * half
        positive = jnp.sum(positive, axis=0, keepdims=True)
        pos_grad = -jax.nn.sigmoid(-positive) * live
        for c in range(PART // 32):
            rows = slice(c * 32, (c + 1) * 32)
            ids = c * 32 + lax.broadcasted_iota(jnp.int32, (32, SPAN), 0)
            high, low = split(score[rows] + jnp.where(ids == tail_row, pos_grad, 0.0))
            c_high[rows] = high
            c_low[rows] = low
        both = mm(r_split[...], c_high[...])
        q_t = both[:D] + both[D:] + mm(r_split[0:D], c_low[...])
        high, low = split(q_t * h_t)
        z_ref[k, 0:D] = high
        z_ref[k, D : 2 * D] = low
        high, low = split(q_t * w_t)
        cat[0:D] = high
        cat[D : 2 * D] = low
        both = mm_nt(cat[...], hot[...])
        grad = both[:D] + both[D:]
        acc = ls_out[...] + jnp.mean(grad * grad, axis=0, keepdims=True)
        ls_out[...] = acc
        set_left(lt[...] - grad * (0.1 * lax.rsqrt(acc)))
        both = mm_nt(s3[0 : 2 * D], c_high[...])
        grad = both[:D] + both[D:] + mm_nt(s3[0:D], c_low[...])
        acc = rs_out[...] + jnp.mean(grad * grad, axis=0, keepdims=True)
        rs_out[...] = acc
        set_right(rt[...] - grad * (0.1 * lax.rsqrt(acc)))
        return 0

    lax.fori_loop(0, block_turns(count_ref), one, 0)
    if second:
        l_out[...] = lt[...].T
        r_out[...] = rt[...].T
    else:
        l_out[...] = lt[...]
        r_out[0:D, :] = rt[...]
        r_out[D : D + 8, :] = jnp.broadcast_to(rs_out[...], (8, PART))


def params():
    return pltpu.CompilerParams(vmem_limit_bytes=56 * 1024 * 1024)


def gather_rows(count, rel, ops):
    return pl.pallas_call(
        gather_kernel,
        out_shape=jax.ShapeDtypeStruct((8, D, SPAN), jnp.float32),
        in_specs=[SMEM, VMEM, VMEM],
        out_specs=VMEM,
        scratch_shapes=[pltpu.VMEM((REL, SPAN), jnp.bfloat16), pltpu.VMEM((2 * D, REL), jnp.bfloat16)],
        compiler_params=params(),
        cost_estimate=pl.CostEstimate(flops=8 * 4 * REL * SPAN * D, bytes_accessed=6 * 2**20, transcendentals=0),
        name="gather_operators",
    )(count, rel, ops)


def relation_grads(count1, count2, rel1, rel2, z1, z2):
    return pl.pallas_call(
        grads_kernel,
        out_shape=jax.ShapeDtypeStruct((REL, D), jnp.float32),
        in_specs=[SMEM, SMEM, VMEM, VMEM, VMEM, VMEM],
        out_specs=VMEM,
        scratch_shapes=[pltpu.VMEM((REL, SPAN), jnp.bfloat16), pltpu.VMEM((REL, 2 * D), jnp.float32)],
        compiler_params=params(),
        name="relation_grads",
    )(count1, count2, rel1, rel2, z1, z2)


def train(second, count, heads, tails, negs, w, left, left_state, right, right_state):
    f32, bf16 = jnp.float32, jnp.bfloat16
    if second:
        shapes = [((PART, D), f32), ((1, PART), f32), ((PART, D), f32), ((1, PART), f32)]
    else:
        shapes = [((D, PART), f32), ((1, PART), f32), ((D + 8, PART), f32), ((1, PART), f32)]
    shapes.append(((8, 2 * D, SPAN), bf16))
    return pl.pallas_call(
        lambda *refs: train_kernel(second, *refs),
        out_shape=[jax.ShapeDtypeStruct(*s) for s in shapes],
        in_specs=[SMEM] + [VMEM] * 8,
        out_specs=[VMEM] * 5,
        scratch_shapes=[
            pltpu.VMEM((D, PART), f32),
            pltpu.VMEM((D, PART), f32),
            pltpu.VMEM((2 * D, PART), bf16),
            pltpu.VMEM((2 * D, PART), bf16),
            pltpu.VMEM((PART, 3 * D), bf16),
            pltpu.VMEM((PART, SPAN), bf16),
            pltpu.VMEM((3 * D, SPAN), bf16),
            pltpu.VMEM((2 * D, SPAN), bf16),
            pltpu.VMEM((PART, SPAN), f32),
            pltpu.VMEM((PART, SPAN), bf16),
            pltpu.VMEM((PART, SPAN), bf16),
        ],
        compiler_params=params(),
        name="train_second" if second else "train_first",
    )(count, heads, tails, negs, w, left, left_state, right, right_state)


def exchange(x, mask):
    return lax.ppermute(x, AXES, [(i, i ^ mask) for i in range(256)])


def gather_all(x):
    x = x.reshape(1, 18, 128)
    for masks in STAGES:
        x = jnp.concatenate([x] + [exchange(x, m) for m in masks], axis=0)
    return x.reshape(REL, D)


def scatter_sum(g):
    g = g.reshape(256, 18, 128)
    for masks in STAGES[::-1]:
        n = g.shape[0] // (len(masks) + 1)
        total = g[:n]
        for j, m in enumerate(masks):
            total = total + exchange(g[(j + 1) * n : (j + 2) * n], m)
        g = total
    return g.reshape(9, D)


def row_positions(relations):
    me = lax.axis_index(AXES)
    owner = relations * 7282 >> 16
    away = owner ^ me
    place = (
        (away & 7)
        | (away >> 4 & 3) << 3
        | (away >> 3 & 1) << 5
        | (away >> 7 & 1) << 6
        | (away >> 6 & 1) << 7
    )
    return place * 9 + (relations - owner * 9)


def move(right, mask):
    branches = [
        (lambda x, m=m: lax.ppermute(x, "dom", [(i, i ^ m) for i in range(64)])) for m in range(1, 64)
    ]
    return lax.switch(mask - 1, branches, right)


def body(left_table, left_state, right_table, right_state, operators, operator_state,
         heads, tails, relations, negatives, edge_counts, partner_mask):
    ops = gather_all(operators)
    rel = row_positions(relations).reshape(2, 8, SPAN)
    heads = heads.reshape(2, 8, SPAN)
    tails = tails.reshape(2, 8, SPAN)
    w1 = gather_rows(edge_counts[0], rel[0], ops)
    left, ls, right, _, z1 = train(
        False, edge_counts[0], heads[0], tails[0], negatives[0], w1,
        left_table, left_state.reshape(1, PART), right_table, right_state.reshape(1, PART),
    )
    w2 = gather_rows(edge_counts[1], rel[1], ops)
    right = move(right, partner_mask[0])
    left, ls, right, rs, z2 = train(
        True, edge_counts[1], heads[1], tails[1], negatives[1], w2, left, ls, right, ls
    )
    grads = scatter_sum(relation_grads(edge_counts[0], edge_counts[1], rel[0], rel[1], z1, z2))
    new_acc = operator_state + grads * grads
    new_operators = operators - 0.5 * grads / jnp.sqrt(new_acc)
    return left, ls.reshape(PART), right, rs.reshape(PART), new_operators


def solution(mesh):
    whole = P(AXES)
    placed = (
        P(AXES, None), whole, P(AXES, None), whole, P(AXES, None), P(AXES, None),
        P(None, AXES), P(None, AXES), P(None, AXES), P(None, AXES, None), P(None, AXES), P(),
    )
    return jax.shard_map(
        body,
        mesh=mesh,
        in_specs=placed,
        out_specs=(P(AXES, None), whole, P(AXES, None), whole, P(AXES, None)),
        check_vma=False,
    )
```

```python
import jax
import jax.numpy as jnp
from jax import lax
from jax.experimental import pallas as pl
from jax.experimental.pallas import tpu as pltpu
from jax.sharding import PartitionSpec as P

D = 256
PART = 1024
SPAN = 512
REL = 2304
VMEM = pl.BlockSpec(memory_space=pltpu.VMEM)
SMEM = pl.BlockSpec(memory_space=pltpu.SMEM)
AXES = ("grp", "dom")
Z, X, Y, CORE = 0x07, 0x30, 0x88, 0x40


def split(x):
    high = x.astype(jnp.bfloat16)
    return high, (x - high.astype(jnp.float32)).astype(jnp.bfloat16)


def mm(x, y):
    return jnp.dot(x, y, preferred_element_type=jnp.float32)


def mm_nt(x, y):
    return lax.dot_general(x, y, (((1,), (1,)), ((), ())), preferred_element_type=jnp.float32)


def block_turns(count_ref, turn):
    return (count_ref[turn, 0] + SPAN - 1) // SPAN


def row_of(ref, turn, k):
    return ref[turn : turn + 1, pl.ds(pl.multiple_of(k * SPAN, SPAN), SPAN)]


def one_hot(rows, index_row, base=0):
    ids = base + lax.broadcasted_iota(jnp.int32, (rows, SPAN), 0)
    return jnp.where(ids == index_row, 1.0, 0.0).astype(jnp.bfloat16)


def load_operators(ops_split, mine_ref, other_ref):
    for c in range(REL // 256):
        for half, ops_ref in enumerate((mine_ref, other_ref)):
            rows = slice(c * 256 + half * 128, c * 256 + half * 128 + 128)
            high, low = split(ops_ref[:, c * 256 : (c + 1) * 256].T)
            ops_split[0:D, rows] = high
            ops_split[D : 2 * D, rows] = low


def set_hot(hot, index_row):
    for c in range(hot.shape[0] // 256):
        hot[c * 256 : (c + 1) * 256] = one_hot(256, index_row, c * 256)


def operators_part(index_row, c, n, hot, ops_split):
    for j in range(c, c + n):
        hot[j * 256 : (j + 1) * 256] = one_hot(256, index_row, j * 256)
    both = mm(ops_split[:, c * 256 : (c + n) * 256], hot[c * 256 : (c + n) * 256])
    return both[:D] + both[D:]


def add_grads_part(index_row, c, n, hot, z, acc):
    rows = slice(c * 256, (c + n) * 256)
    for j in range(c, c + n):
        hot[j * 256 : (j + 1) * 256] = one_hot(256, index_row, j * 256)
    both = mm_nt(hot[rows], z)
    acc[rows] += both[:, :D] + both[:, D:]


def gather_kernel(turn, count_ref, rel_ref, split_ref, w_ref):
    def one(k, _):
        index_row = row_of(rel_ref, turn, k)
        w_ref[k] = jnp.zeros((D, SPAN), jnp.float32)

        def part(c, _):
            start = pl.multiple_of(c * 256, 256)
            both = mm(split_ref[:, pl.ds(start, 256)], one_hot(256, index_row, start))
            w_ref[k] += both[:D] + both[D:]
            return 0

        return lax.fori_loop(0, REL // 256, part, 0)

    lax.fori_loop(0, block_turns(count_ref, turn), one, 0)


def grads_kernel(turn, count_ref, rel_ref, z_ref, g_ref):
    def clear(c, _):
        g_ref[pl.ds(pl.multiple_of(c * 256, 256), 256), :] = jnp.zeros((256, D), jnp.float32)
        return 0

    lax.fori_loop(0, REL // 256, clear, 0)

    def one(k, _):
        index_row = row_of(rel_ref, turn, k)

        def part(c, _):
            start = pl.multiple_of(c * 256, 256)
            both = mm_nt(one_hot(256, index_row, start), z_ref[k])
            g_ref[pl.ds(start, 256), :] += both[:, :D] + both[:, D:]
            return 0

        return lax.fori_loop(0, REL // 256, part, 0)

    lax.fori_loop(0, block_turns(count_ref, turn), one, 0)


def train_kernel(second, count_ref, heads_ref, tails_ref, negs_ref, rel_ref, l_ref, ls_ref, r_ref, rs_ref,
                 x_ref, y_ref, l_out, ls_out, r_out, rs_out, u_out, v_out,
                 lt, rt, l_split, r_split, r_cols, hot, s3, cat, score, c_high, c_low,
                 h_now, w_now, rel_hot, *sums):
    turn = 1 if second else 0

    def set_left(value):
        lt[...] = value
        high, low = split(value)
        l_split[0:D] = high
        l_split[D : 2 * D] = low

    def set_right(value):
        rt[...] = value
        high, low = split(value)
        r_split[0:D] = high
        r_split[D : 2 * D] = low
        across = value.T
        high, low = split(across)
        r_cols[:, 0:D] = high
        r_cols[:, D : 2 * D] = high
        r_cols[:, 2 * D : 3 * D] = low

    def set_heads(k, w_t):
        set_hot(hot, row_of(heads_ref, turn, k))
        both = mm(l_split[...], hot[...])
        h_t = both[:D] + both[D:]
        h_now[...] = h_t
        w_now[...] = w_t
        s_high, s_low = split(h_t * w_t)
        s3[0:D] = s_high
        s3[D : 2 * D] = s_low
        s3[2 * D : 3 * D] = s_high

    if second:
        set_left(l_ref[...])
        set_right(r_ref[0:D, :])
        rs_out[...] = r_ref[D : D + 1, :]
        rel_acc, z_last = sums
        rel_acc[...] = y_ref[...]
        z_last[...] = jnp.zeros_like(z_last)
        set_heads(0, x_ref[0])
    else:
        load_operators(v_out, x_ref, y_ref)
        set_left(l_ref[...].T)
        set_right(r_ref[...].T)
        rs_out[...] = rs_ref[...]
        set_heads(0, operators_part(row_of(rel_ref, turn, 0), 0, 9, rel_hot, v_out))
    ls_out[...] = ls_ref[...]
    count = count_ref[turn, 0]

    def one(k, _):
        following = jnp.minimum(k + 1, 7)
        tail_row = row_of(tails_ref, turn, k)
        neg_row = negs_ref[turn, pl.ds(k, 1), :]
        slots = k * SPAN + lax.broadcasted_iota(jnp.int32, (1, SPAN), 1)
        live = jnp.where(slots < count, 1.0, 0.0)
        half = live * (0.5 / SPAN)
        score[...] = mm(r_cols[...], s3[...])
        rel_row = row_of(rel_ref, turn, jnp.maximum(k - 1, 0) if second else following)

        def beside(c, n):
            if second:
                add_grads_part(rel_row, c, n, rel_hot, z_last[...], rel_acc)
                return 0.0
            return operators_part(rel_row, c, n, rel_hot, v_out)

        w_next = beside(0, 3)
        positive = jnp.zeros((8, SPAN), jnp.float32)
        for c in range(PART // 32):
            rows = slice(c * 32, (c + 1) * 32)
            ids = c * 32 + lax.broadcasted_iota(jnp.int32, (32, SPAN), 0)
            a = score[rows]
            times = jnp.sum(jnp.where(ids == neg_row, 1.0, 0.0), axis=1, keepdims=True)
            picked = jnp.where(ids == tail_row, a, 0.0)
            positive = positive + (picked[0:8] + picked[8:16]) + (picked[16:24] + picked[24:32])
            score[rows] = (jnp.tanh(0.5 * a) + 1.0) * times * half
        positive = jnp.sum(positive, axis=0, keepdims=True)
        w_next = w_next + beside(3, 3)
        pos_grad = -jax.nn.sigmoid(-positive) * live
        for c in range(PART // 32):
            rows = slice(c * 32, (c + 1) * 32)
            ids = c * 32 + lax.broadcasted_iota(jnp.int32, (32, SPAN), 0)
            high, low = split(score[rows] + jnp.where(ids == tail_row, pos_grad, 0.0))
            c_high[rows] = high
            c_low[rows] = low
        both = mm(r_split[...], c_high[...])
        q_t = both[:D] + both[D:] + mm(r_split[0:D], c_low[...])
        high, low = split(q_t * w_now[...])
        cat[0:D] = high
        cat[D : 2 * D] = low
        z_t = jnp.concatenate(split(q_t * h_now[...]), axis=0)
        both = mm_nt(cat[...], hot[...])
        grad = both[:D] + both[D:]
        acc = ls_out[...] + jnp.mean(grad * grad, axis=0, keepdims=True)
        ls_out[...] = acc
        set_left(lt[...] - grad * (0.1 * lax.rsqrt(acc)))
        both = mm_nt(s3[0 : 2 * D], c_high[...])
        grad = both[:D] + both[D:] + mm_nt(s3[0:D], c_low[...])
        w_next = w_next + beside(6, 3)
        if second:
            z_last[...] = z_t
            w_next = x_ref[following]
        else:
            u_out[k] = z_t
        set_heads(following, w_next)
        acc = rs_out[...] + jnp.mean(grad * grad, axis=0, keepdims=True)
        rs_out[...] = acc
        set_right(rt[...] - grad * (0.1 * lax.rsqrt(acc)))
        return 0

    turns = block_turns(count_ref, turn)
    lax.fori_loop(0, turns, one, 0)
    if second:
        add_grads_part(row_of(rel_ref, turn, turns - 1), 0, 9, rel_hot, z_last[...], rel_acc)
        l_out[...] = lt[...].T
        r_out[...] = rt[...].T
        for c in range(REL // 256):
            rows = slice(c * 256, c * 256 + 128)
            u_out[:, c * 256 : (c + 1) * 256] = rel_acc[rows]
            rows = slice(c * 256 + 128, c * 256 + 256)
            v_out[:, c * 256 : (c + 1) * 256] = rel_acc[rows]
    else:
        l_out[...] = lt[...]
        r_out[0:D, :] = rt[...]
        r_out[D : D + 8, :] = jnp.broadcast_to(rs_out[...], (8, PART))


def params():
    return pltpu.CompilerParams(vmem_limit_bytes=56 * 1024 * 1024)


def cost(flops):
    return pl.CostEstimate(flops=flops, bytes_accessed=8 * 2**20, transcendentals=0)


def gather_rows(turn, count, rel, ops_split):
    return pl.pallas_call(
        lambda *refs: gather_kernel(turn, *refs),
        out_shape=jax.ShapeDtypeStruct((8, D, SPAN), jnp.float32),
        in_specs=[SMEM, VMEM, VMEM],
        out_specs=VMEM,
        compiler_params=params(),
        cost_estimate=cost(8 * 4 * REL * SPAN * D),
        name="gather_operators",
    )(count, rel, ops_split)


def relation_grads(turn, count, rel, z):
    return pl.pallas_call(
        lambda *refs: grads_kernel(turn, *refs),
        out_shape=jax.ShapeDtypeStruct((REL, D), jnp.float32),
        in_specs=[SMEM, VMEM, VMEM],
        out_specs=VMEM,
        compiler_params=params(),
        cost_estimate=cost(8 * 4 * REL * SPAN * D),
        name="relation_grads",
    )(count, rel, z)


def train(second, count, heads, tails, negs, rel, left, left_state, right, right_state, x, y):
    f32, bf16 = jnp.float32, jnp.bfloat16
    sums = []
    if second:
        shapes = [((PART, D), f32), ((1, PART), f32), ((PART, D), f32), ((1, PART), f32)]
        shapes += [((128, REL), f32), ((128, REL), f32)]
        sums = [pltpu.VMEM((REL, D), f32), pltpu.VMEM((2 * D, SPAN), bf16)]
    else:
        shapes = [((D, PART), f32), ((1, PART), f32), ((D + 8, PART), f32), ((1, PART), f32)]
        shapes += [((8, 2 * D, SPAN), bf16), ((2 * D, REL), bf16)]
    return pl.pallas_call(
        lambda *refs: train_kernel(second, *refs),
        out_shape=[jax.ShapeDtypeStruct(*s) for s in shapes],
        in_specs=[SMEM] + [VMEM] * 10,
        out_specs=[VMEM] * 6,
        scratch_shapes=[
            pltpu.VMEM((D, PART), f32),
            pltpu.VMEM((D, PART), f32),
            pltpu.VMEM((2 * D, PART), bf16),
            pltpu.VMEM((2 * D, PART), bf16),
            pltpu.VMEM((PART, 3 * D), bf16),
            pltpu.VMEM((PART, SPAN), bf16),
            pltpu.VMEM((3 * D, SPAN), bf16),
            pltpu.VMEM((2 * D, SPAN), bf16),
            pltpu.VMEM((PART, SPAN), f32),
            pltpu.VMEM((PART, SPAN), bf16),
            pltpu.VMEM((PART, SPAN), bf16),
            pltpu.VMEM((D, SPAN), f32),
            pltpu.VMEM((D, SPAN), f32),
            pltpu.VMEM((REL, SPAN), bf16),
        ]
        + sums,
        compiler_params=params(),
        name="train_second" if second else "train_first",
    )(count, heads, tails, negs, rel, left, left_state, right, right_state, x, y)


def exchange(x, mask):
    return lax.ppermute(x, AXES, [(i, i ^ mask) for i in range(256)])


def trade(x, bits):
    groups = [[i | j for j in range(256) if j & ~bits == 0] for i in range(256) if i & bits == 0]
    return lax.all_to_all(x, AXES, 0, 0, tiled=True, axis_index_groups=groups)


def spread(x, bits, n):
    return trade(jnp.broadcast_to(x[None], (n,) + x.shape).reshape(-1, REL), bits)


def gather_all(x):
    x = spread(spread(spread(x.reshape(1, REL), Z, 8), X, 4), Y, 4)
    return x, exchange(x, CORE)


def scatter_sum(kept, sent):
    g = kept + exchange(sent, CORE)
    for bits, n in ((Y, 4), (X, 4), (Z, 8)):
        g = trade(g, bits).reshape(n, -1, REL).sum(axis=0)
    return g.reshape(9, D)


def row_positions(relations):
    me = lax.axis_index(AXES)
    owner = relations * 7282 >> 16
    place = (
        (owner & 7)
        | (owner >> 4 & 3) << 3
        | (owner >> 3 & 1) << 5
        | (owner >> 7 & 1) << 6
        | ((owner ^ me) >> 6 & 1) << 7
    )
    return (relations - owner * 9) * 256 + place


def move(mask, unit, right, beside, operands):
    def go(right, operands, m):
        moved = right
        if m:
            moved = lax.ppermute(right, "dom", [(i, i ^ m) for i in range(64)])
        return moved, beside(*operands)

    branches = [(lambda x, o, m=m: go(x, o, m)) for m in range(0, 8 * unit, unit)]
    return lax.switch(mask // unit & 7, branches, right, operands)


def body(left_table, left_state, right_table, right_state, operators, operator_state,
         heads, tails, relations, negatives, edge_counts, partner_mask):
    mine, other = gather_all(operators)
    rel = row_positions(relations)
    lists = (edge_counts, heads, tails, negatives, rel)
    left, ls, right, _, z, ops_split = train(
        False, *lists, left_table, left_state.reshape(1, PART), right_table, right_state.reshape(1, PART), mine, other
    )
    mask = partner_mask[0]
    right, w = move(mask, 1, right, lambda *x: gather_rows(1, *x), (edge_counts, rel, ops_split))
    right, g = move(mask, 8, right, lambda *x: relation_grads(0, *x), (edge_counts, rel, z))
    left, ls, right, rs, kept, sent = train(True, *lists, left, ls, right, ls, w, g)
    grads = scatter_sum(kept, sent)
    new_acc = operator_state + grads * grads
    new_operators = operators - 0.5 * grads / jnp.sqrt(new_acc)
    return left, ls.reshape(PART), right, rs.reshape(PART), new_operators


def solution(mesh):
    whole = P(AXES)
    placed = (
        P(AXES, None), whole, P(AXES, None), whole, P(AXES, None), P(AXES, None),
        P(None, AXES), P(None, AXES), P(None, AXES), P(None, AXES, None), P(None, AXES), P(),
    )
    return jax.shard_map(
        body,
        mesh=mesh,
        in_specs=placed,
        out_specs=(P(AXES, None), whole, P(AXES, None), whole, P(AXES, None)),
        check_vma=False,
    )
```

```python
import jax
import jax.numpy as jnp
from jax import lax
from jax.experimental import pallas as pl
from jax.experimental.pallas import tpu as pltpu
from jax.sharding import PartitionSpec as P

D = 256
PART = 1024
SPAN = 512
REL = 2304
VMEM = pl.BlockSpec(memory_space=pltpu.VMEM)
SMEM = pl.BlockSpec(memory_space=pltpu.SMEM)
AXES = ("grp", "dom")
CUT = 5
Z, X, Y, CORE = 0x07, (16, 32, 48), (8, 128, 136), 64


def split(x):
    high = x.astype(jnp.bfloat16)
    return high, (x - high.astype(jnp.float32)).astype(jnp.bfloat16)


def mm(x, y):
    return jnp.dot(x, y, preferred_element_type=jnp.float32)


def mm_nt(x, y):
    return lax.dot_general(x, y, (((1,), (1,)), ((), ())), preferred_element_type=jnp.float32)


def block_turns(count_ref, turn):
    return (count_ref[turn, 0] + SPAN - 1) // SPAN


def row_of(ref, turn, k):
    return ref[turn : turn + 1, pl.ds(pl.multiple_of(k * SPAN, SPAN), SPAN)]


def one_hot(rows, index_row, base=0):
    ids = base + lax.broadcasted_iota(jnp.int32, (rows, SPAN), 0)
    return jnp.where(ids == index_row, 1.0, 0.0).astype(jnp.bfloat16)


def load_operators(ops_split, pieces):
    for c in range(REL // 256):
        side, column = (0, c) if c < CUT else (1, c - CUT)
        for half in range(2):
            rows = slice(c * 256 + half * 128, c * 256 + half * 128 + 128)
            high, low = split(pieces[2 * half + side][:, column * 256 : (column + 1) * 256].T)
            ops_split[0:D, rows] = high
            ops_split[D : 2 * D, rows] = low


def set_hot(hot, index_row):
    for c in range(hot.shape[0] // 256):
        hot[c * 256 : (c + 1) * 256] = one_hot(256, index_row, c * 256)


def operators_part(index_row, c, n, hot, ops_split):
    for j in range(c, c + n):
        hot[j * 256 : (j + 1) * 256] = one_hot(256, index_row, j * 256)
    both = mm(ops_split[:, c * 256 : (c + n) * 256], hot[c * 256 : (c + n) * 256])
    return both[:D] + both[D:]


def add_grads_part(index_row, c, n, hot, z, acc):
    rows = slice(c * 256, (c + n) * 256)
    for j in range(c, c + n):
        hot[j * 256 : (j + 1) * 256] = one_hot(256, index_row, j * 256)
    both = mm_nt(hot[rows], z)
    acc[rows] += both[:, :D] + both[:, D:]


def gather_kernel(turn, count_ref, rel_ref, split_ref, w_ref):
    def one(k, _):
        index_row = row_of(rel_ref, turn, k)
        w_ref[k] = jnp.zeros((D, SPAN), jnp.float32)

        def part(c, _):
            start = pl.multiple_of(c * 256, 256)
            both = mm(split_ref[:, pl.ds(start, 256)], one_hot(256, index_row, start))
            w_ref[k] += both[:D] + both[D:]
            return 0

        return lax.fori_loop(0, REL // 256, part, 0)

    lax.fori_loop(0, block_turns(count_ref, turn), one, 0)


def grads_kernel(turn, count_ref, rel_ref, z_ref, g_ref):
    def clear(c, _):
        g_ref[pl.ds(pl.multiple_of(c * 256, 256), 256), :] = jnp.zeros((256, D), jnp.float32)
        return 0

    lax.fori_loop(0, REL // 256, clear, 0)

    def one(k, _):
        index_row = row_of(rel_ref, turn, k)

        def part(c, _):
            start = pl.multiple_of(c * 256, 256)
            both = mm_nt(one_hot(256, index_row, start), z_ref[k])
            g_ref[pl.ds(start, 256), :] += both[:, :D] + both[:, D:]
            return 0

        return lax.fori_loop(0, REL // 256, part, 0)

    lax.fori_loop(0, block_turns(count_ref, turn), one, 0)


def train_kernel(second, count_ref, heads_ref, tails_ref, negs_ref, rel_ref, l_ref, ls_ref, r_ref, rs_ref,
                 *rest):
    if second:
        (x_ref, y_ref, l_out, ls_out, r_out, rs_out), g_out, rest = rest[:6], rest[6:10], rest[10:]
        rel_acc, z_last = rest[-2:]
        rest = rest[:-2]
    else:
        pieces, (l_out, ls_out, r_out, rs_out, u_out, v_out), rest = rest[:4], rest[4:10], rest[10:]
    (lt, rt, l_split, r_split, r_cols, hot, s3, cat, score, c_high, c_low,
     h_now, w_now, rel_hot) = rest
    turn = 1 if second else 0

    def set_left(value):
        lt[...] = value
        high, low = split(value)
        l_split[0:D] = high
        l_split[D : 2 * D] = low

    def set_right(value):
        rt[...] = value
        high, low = split(value)
        r_split[0:D] = high
        r_split[D : 2 * D] = low
        high, low = high.T, low.T
        r_cols[:, 0:D] = high
        r_cols[:, D : 2 * D] = high
        r_cols[:, 2 * D : 3 * D] = low

    def set_heads(k, w_t):
        set_hot(hot, row_of(heads_ref, turn, k))
        both = mm(l_split[...], hot[...])
        h_t = both[:D] + both[D:]
        h_now[...] = h_t
        w_now[...] = w_t
        s_high, s_low = split(h_t * w_t)
        s3[0:D] = s_high
        s3[D : 2 * D] = s_low
        s3[2 * D : 3 * D] = s_high

    if second:
        set_left(l_ref[...])
        set_right(r_ref[0:D, :])
        rs_out[...] = r_ref[D : D + 1, :]
        rel_acc[...] = y_ref[...]
        z_last[...] = jnp.zeros_like(z_last)
        set_heads(0, x_ref[0])
    else:
        load_operators(v_out, pieces)
        set_left(l_ref[...].T)
        set_right(r_ref[...].T)
        rs_out[...] = rs_ref[...]
        set_heads(0, operators_part(row_of(rel_ref, turn, 0), 0, 9, rel_hot, v_out))
    ls_out[...] = ls_ref[...]
    count = count_ref[turn, 0]

    def one(k, _):
        following = jnp.minimum(k + 1, 7)
        tail_row = row_of(tails_ref, turn, k)
        neg_row = negs_ref[turn, pl.ds(k, 1), :]
        slots = k * SPAN + lax.broadcasted_iota(jnp.int32, (1, SPAN), 1)
        live = jnp.where(slots < count, 1.0, 0.0)
        half = live * (0.5 / SPAN)
        score[...] = mm(r_cols[...], s3[...])
        rel_row = row_of(rel_ref, turn, jnp.maximum(k - 1, 0) if second else following)

        def beside(c, n):
            if second:
                add_grads_part(rel_row, c, n, rel_hot, z_last[...], rel_acc)
                return 0.0
            return operators_part(rel_row, c, n, rel_hot, v_out)

        w_next = beside(0, 3)
        positive = jnp.zeros((8, SPAN), jnp.float32)
        for c in range(PART // 32):
            rows = slice(c * 32, (c + 1) * 32)
            ids = c * 32 + lax.broadcasted_iota(jnp.int32, (32, SPAN), 0)
            a = score[rows]
            times = jnp.sum(jnp.where(ids == neg_row, 1.0, 0.0), axis=1, keepdims=True)
            picked = jnp.where(ids == tail_row, a, 0.0)
            positive = positive + (picked[0:8] + picked[8:16]) + (picked[16:24] + picked[24:32])
            score[rows] = (jnp.tanh(0.5 * a) + 1.0) * times * half
        positive = jnp.sum(positive, axis=0, keepdims=True)
        w_next = w_next + beside(3, 3)
        pos_grad = -jax.nn.sigmoid(-positive) * live
        for c in range(PART // 32):
            rows = slice(c * 32, (c + 1) * 32)
            ids = c * 32 + lax.broadcasted_iota(jnp.int32, (32, SPAN), 0)
            high, low = split(score[rows] + jnp.where(ids == tail_row, pos_grad, 0.0))
            c_high[rows] = high
            c_low[rows] = low
        both = mm(r_split[...], c_high[...])
        q_t = both[:D] + both[D:] + mm(r_split[0:D], c_low[...])
        high, low = split(q_t * w_now[...])
        cat[0:D] = high
        cat[D : 2 * D] = low
        z_t = jnp.concatenate(split(q_t * h_now[...]), axis=0)
        both = mm_nt(cat[...], hot[...])
        grad = both[:D] + both[D:]
        acc = ls_out[...] + jnp.mean(grad * grad, axis=0, keepdims=True)
        ls_out[...] = acc
        set_left(lt[...] - grad * (0.1 * lax.rsqrt(acc)))
        both = mm_nt(s3[0 : 2 * D], c_high[...])
        grad = both[:D] + both[D:] + mm_nt(s3[0:D], c_low[...])
        w_next = w_next + beside(6, 3)
        if second:
            z_last[...] = z_t
            w_next = x_ref[following]
        else:
            u_out[k] = z_t
        set_heads(following, w_next)
        acc = rs_out[...] + jnp.mean(grad * grad, axis=0, keepdims=True)
        rs_out[...] = acc
        set_right(rt[...] - grad * (0.1 * lax.rsqrt(acc)))
        return 0

    turns = block_turns(count_ref, turn)
    lax.fori_loop(0, turns, one, 0)
    if second:
        add_grads_part(row_of(rel_ref, turn, turns - 1), 0, 9, rel_hot, z_last[...], rel_acc)
        l_out[...] = lt[...].T
        r_out[...] = rt[...].T
        for c in range(REL // 256):
            side, column = (0, c) if c < CUT else (1, c - CUT)
            for half in range(2):
                rows = slice(c * 256 + half * 128, c * 256 + half * 128 + 128)
                g_out[2 * half + side][:, column * 256 : (column + 1) * 256] = rel_acc[rows]
    else:
        l_out[...] = lt[...]
        r_out[0:D, :] = rt[...]
        r_out[D : D + 8, :] = jnp.broadcast_to(rs_out[...], (8, PART))


def params():
    return pltpu.CompilerParams(vmem_limit_bytes=56 * 1024 * 1024)


def cost(flops):
    return pl.CostEstimate(flops=flops, bytes_accessed=8 * 2**20, transcendentals=0)


def gather_rows(turn, count, rel, ops_split):
    return pl.pallas_call(
        lambda *refs: gather_kernel(turn, *refs),
        out_shape=jax.ShapeDtypeStruct((8, D, SPAN), jnp.float32),
        in_specs=[SMEM, VMEM, VMEM],
        out_specs=VMEM,
        compiler_params=params(),
        cost_estimate=cost(8 * 4 * REL * SPAN * D),
        name="gather_operators",
    )(count, rel, ops_split)


def relation_grads(turn, count, rel, z):
    return pl.pallas_call(
        lambda *refs: grads_kernel(turn, *refs),
        out_shape=jax.ShapeDtypeStruct((REL, D), jnp.float32),
        in_specs=[SMEM, VMEM, VMEM],
        out_specs=VMEM,
        compiler_params=params(),
        cost_estimate=cost(8 * 4 * REL * SPAN * D),
        name="relation_grads",
    )(count, rel, z)


def train(second, count, heads, tails, negs, rel, left, left_state, right, right_state, *others):
    f32, bf16 = jnp.float32, jnp.bfloat16
    sums = []
    if second:
        shapes = [((PART, D), f32), ((1, PART), f32), ((PART, D), f32), ((1, PART), f32)]
        shapes += [((128, CUT * D), f32), ((128, REL - CUT * D), f32)] * 2
        sums = [pltpu.VMEM((REL, D), f32), pltpu.VMEM((2 * D, SPAN), bf16)]
    else:
        shapes = [((D, PART), f32), ((1, PART), f32), ((D + 8, PART), f32), ((1, PART), f32)]
        shapes += [((8, 2 * D, SPAN), bf16), ((2 * D, REL), bf16)]
    return pl.pallas_call(
        lambda *refs: train_kernel(second, *refs),
        out_shape=[jax.ShapeDtypeStruct(*s) for s in shapes],
        in_specs=[SMEM] + [VMEM] * (8 + len(others)),
        out_specs=[VMEM] * len(shapes),
        scratch_shapes=[
            pltpu.VMEM((D, PART), f32),
            pltpu.VMEM((D, PART), f32),
            pltpu.VMEM((2 * D, PART), bf16),
            pltpu.VMEM((2 * D, PART), bf16),
            pltpu.VMEM((PART, 3 * D), bf16),
            pltpu.VMEM((PART, SPAN), bf16),
            pltpu.VMEM((3 * D, SPAN), bf16),
            pltpu.VMEM((2 * D, SPAN), bf16),
            pltpu.VMEM((PART, SPAN), f32),
            pltpu.VMEM((PART, SPAN), bf16),
            pltpu.VMEM((PART, SPAN), bf16),
            pltpu.VMEM((D, SPAN), f32),
            pltpu.VMEM((D, SPAN), f32),
            pltpu.VMEM((REL, SPAN), bf16),
        ]
        + sums,
        compiler_params=params(),
        name="train_second" if second else "train_first",
    )(count, heads, tails, negs, rel, left, left_state, right, right_state, *others)


def exchange(x, mask):
    return lax.ppermute(x, AXES, [(i, i ^ mask) for i in range(256)])


def trade(x, bits):
    groups = [[i | j for j in range(256) if j & ~bits == 0] for i in range(256) if i & bits == 0]
    return lax.all_to_all(x, AXES, 0, 0, tiled=True, axis_index_groups=groups)


def gather_over(x, masks):
    return jnp.concatenate([x] + [exchange(x, m) for m in masks], axis=0)


def sum_over(g, masks):
    n = g.shape[0] // (len(masks) + 1)
    total = g[:n]
    for j, m in enumerate(masks):
        total = total + exchange(g[(j + 1) * n : (j + 2) * n], m)
    return total


def gather_all(x):
    x = trade(jnp.broadcast_to(x.reshape(1, REL), (8, REL)), Z)
    first, last = x[:, : CUT * D], x[:, CUT * D :]
    first, last = gather_over(first, X), gather_over(last, Y)
    first, last = gather_over(first, Y), gather_over(last, X)
    return first, last, exchange(first, CORE), exchange(last, CORE)


def scatter_sum(first, last, first_sent, last_sent):
    first, last = first + exchange(first_sent, CORE), last + exchange(last_sent, CORE)
    first, last = sum_over(first, Y), sum_over(last, X)
    first, last = sum_over(first, X), sum_over(last, Y)
    return trade(jnp.concatenate([first, last], axis=1), Z).sum(axis=0).reshape(9, D)


def row_positions(relations):
    me = lax.axis_index(AXES)
    owner = relations * 7282 >> 16
    away = owner ^ me
    x = away >> 4 & 3
    y = away >> 3 & 1 | away >> 6 & 2
    piece = relations - owner * 9
    place = (owner & 7) | jnp.where(piece < CUT, x | y << 2, y | x << 2) << 3 | (away >> 6 & 1) << 7
    return piece * 256 + place


def move(mask, unit, right, beside, operands):
    def go(right, operands, m):
        moved = right
        if m:
            moved = lax.ppermute(right, "dom", [(i, i ^ m) for i in range(64)])
        return moved, beside(*operands)

    branches = [(lambda x, o, m=m: go(x, o, m)) for m in range(0, 8 * unit, unit)]
    return lax.switch(mask // unit & 7, branches, right, operands)


def body(left_table, left_state, right_table, right_state, operators, operator_state,
         heads, tails, relations, negatives, edge_counts, partner_mask):
    pieces = gather_all(operators)
    rel = row_positions(relations)
    lists = (edge_counts, heads, tails, negatives, rel)
    left, ls, right, _, z, ops_split = train(
        False, *lists, left_table, left_state.reshape(1, PART), right_table, right_state.reshape(1, PART), *pieces
    )
    mask = partner_mask[0]
    right, w = move(mask, 1, right, lambda *x: gather_rows(1, *x), (edge_counts, rel, ops_split))
    right, g = move(mask, 8, right, lambda *x: relation_grads(0, *x), (edge_counts, rel, z))
    left, ls, right, rs, *sums = train(True, *lists, left, ls, right, ls, w, g)
    grads = scatter_sum(*sums)
    new_acc = operator_state + grads * grads
    new_operators = operators - 0.5 * grads / jnp.sqrt(new_acc)
    return left, ls.reshape(PART), right, rs.reshape(PART), new_operators


def solution(mesh):
    whole = P(AXES)
    placed = (
        P(AXES, None), whole, P(AXES, None), whole, P(AXES, None), P(AXES, None),
        P(None, AXES), P(None, AXES), P(None, AXES), P(None, AXES, None), P(None, AXES), P(),
    )
    return jax.shard_map(
        body,
        mesh=mesh,
        in_specs=placed,
        out_specs=(P(AXES, None), whole, P(AXES, None), whole, P(AXES, None)),
        check_vma=False,
    )
```

```python
import jax
import jax.numpy as jnp
from jax import lax
from jax.experimental import pallas as pl
from jax.experimental.pallas import tpu as pltpu
from jax.sharding import PartitionSpec as P

D = 256
PART = 1024
SPAN = 512
REL = 2304
VMEM = pl.BlockSpec(memory_space=pltpu.VMEM)
SMEM = pl.BlockSpec(memory_space=pltpu.SMEM)
AXES = ("grp", "dom")
CUT = 5
Z, X, Y, CORE = 0x07, (16, 32, 48), (8, 128, 136), 64


def split(x):
    high = x.astype(jnp.bfloat16)
    return high, (x - high.astype(jnp.float32)).astype(jnp.bfloat16)


def mm(x, y):
    return jnp.dot(x, y, preferred_element_type=jnp.float32)


def mm_nt(x, y):
    return lax.dot_general(x, y, (((1,), (1,)), ((), ())), preferred_element_type=jnp.float32)


def block_turns(count_ref, turn):
    return (count_ref[turn, 0] + SPAN - 1) // SPAN


def row_of(ref, turn, k):
    return ref[turn : turn + 1, pl.ds(pl.multiple_of(k * SPAN, SPAN), SPAN)]


def one_hot(rows, index_row, base=0):
    ids = base + lax.broadcasted_iota(jnp.int32, (rows, SPAN), 0)
    return jnp.where(ids == index_row, 1.0, 0.0).astype(jnp.bfloat16)


def load_operators(ops_split, pieces):
    for c in range(REL // 256):
        side, column = (0, c) if c < CUT else (1, c - CUT)
        for half in range(2):
            rows = slice(c * 256 + half * 128, c * 256 + half * 128 + 128)
            high, low = split(pieces[2 * half + side][:, column * 256 : (column + 1) * 256].T)
            ops_split[0:D, rows] = high
            ops_split[D : 2 * D, rows] = low


def set_hot(hot, index_row):
    for c in range(hot.shape[0] // 256):
        hot[c * 256 : (c + 1) * 256] = one_hot(256, index_row, c * 256)


def operators_part(index_row, c, n, hot, ops_split):
    for j in range(c, c + n):
        hot[j * 256 : (j + 1) * 256] = one_hot(256, index_row, j * 256)
    both = mm(ops_split[:, c * 256 : (c + n) * 256], hot[c * 256 : (c + n) * 256])
    return both[:D] + both[D:]


def add_grads_part(index_row, c, n, hot, z, acc):
    rows = slice(c * 256, (c + n) * 256)
    for j in range(c, c + n):
        hot[j * 256 : (j + 1) * 256] = one_hot(256, index_row, j * 256)
    both = mm_nt(hot[rows], z)
    acc[rows] += both[:, :D] + both[:, D:]


def gather_kernel(turn, count_ref, rel_ref, split_ref, w_ref):
    def one(k, _):
        index_row = row_of(rel_ref, turn, k)
        w_ref[k] = jnp.zeros((D, SPAN), jnp.float32)

        def part(c, _):
            start = pl.multiple_of(c * 256, 256)
            both = mm(split_ref[:, pl.ds(start, 256)], one_hot(256, index_row, start))
            w_ref[k] += both[:D] + both[D:]
            return 0

        return lax.fori_loop(0, REL // 256, part, 0)

    lax.fori_loop(0, block_turns(count_ref, turn), one, 0)


def grads_kernel(turn, count_ref, rel_ref, z_ref, g_ref):
    def clear(c, _):
        g_ref[pl.ds(pl.multiple_of(c * 256, 256), 256), :] = jnp.zeros((256, D), jnp.float32)
        return 0

    lax.fori_loop(0, REL // 256, clear, 0)

    def one(k, _):
        index_row = row_of(rel_ref, turn, k)

        def part(c, _):
            start = pl.multiple_of(c * 256, 256)
            both = mm_nt(one_hot(256, index_row, start), z_ref[k])
            g_ref[pl.ds(start, 256), :] += both[:, :D] + both[:, D:]
            return 0

        return lax.fori_loop(0, REL // 256, part, 0)

    lax.fori_loop(0, block_turns(count_ref, turn), one, 0)


def train_kernel(second, count_ref, heads_ref, tails_ref, negs_ref, rel_ref, l_ref, ls_ref, r_ref, rs_ref,
                 *rest):
    if second:
        (x_ref, y_ref, l_out, ls_out, r_out, rs_out), g_out, rest = rest[:6], rest[6:10], rest[10:]
        rel_acc, z_last = rest[-2:]
        rest = rest[:-2]
    else:
        pieces, (l_out, ls_out, r_out, rs_out, u_out, v_out), rest = rest[:4], rest[4:10], rest[10:]
    (lt, rt, l_split, r_split, r_cols, hot, s3, cat, score, c_high, c_low,
     h_now, w_now, rel_hot) = rest
    turn = 1 if second else 0

    def set_left(value):
        lt[...] = value
        high, low = split(value)
        l_split[0:D] = high
        l_split[D : 2 * D] = low

    def set_right(value):
        rt[...] = value
        high, low = split(value)
        r_split[0:D] = high
        r_split[D : 2 * D] = low
        high, low = high.T, low.T
        r_cols[:, 0:D] = high
        r_cols[:, D : 2 * D] = high
        r_cols[:, 2 * D : 3 * D] = low

    def set_heads(k, w_t):
        set_hot(hot, row_of(heads_ref, turn, k))
        both = mm(l_split[...], hot[...])
        h_t = both[:D] + both[D:]
        h_now[...] = h_t
        w_now[...] = w_t
        s_high, s_low = split(h_t * w_t)
        s3[0:D] = s_high
        s3[D : 2 * D] = s_low
        s3[2 * D : 3 * D] = s_high

    if second:
        set_left(l_ref[...])
        set_right(r_ref[0:D, :])
        rs_out[...] = r_ref[D : D + 1, :]
        rel_acc[...] = y_ref[...]
        z_last[...] = jnp.zeros_like(z_last)
        set_heads(0, x_ref[0])
    else:
        load_operators(v_out, pieces)
        set_left(l_ref[...])
        set_right(r_ref[...])
        rs_out[...] = rs_ref[...]
        set_heads(0, operators_part(row_of(rel_ref, turn, 0), 0, 9, rel_hot, v_out))
    ls_out[...] = ls_ref[...]
    count = count_ref[turn, 0]

    def one(k, _):
        following = jnp.minimum(k + 1, 7)
        tail_row = row_of(tails_ref, turn, k)
        neg_row = negs_ref[turn, pl.ds(k, 1), :]
        slots = k * SPAN + lax.broadcasted_iota(jnp.int32, (1, SPAN), 1)
        live = jnp.where(slots < count, 1.0, 0.0)
        half = live * (0.5 / SPAN)
        score[...] = mm(r_cols[...], s3[...])
        rel_row = row_of(rel_ref, turn, jnp.maximum(k - 1, 0) if second else following)

        def beside(c, n):
            if second:
                add_grads_part(rel_row, c, n, rel_hot, z_last[...], rel_acc)
                return 0.0
            return operators_part(rel_row, c, n, rel_hot, v_out)

        w_next = beside(0, 3)
        positive = jnp.zeros((8, SPAN), jnp.float32)
        for c in range(PART // 32):
            rows = slice(c * 32, (c + 1) * 32)
            ids = c * 32 + lax.broadcasted_iota(jnp.int32, (32, SPAN), 0)
            a = score[rows]
            times = jnp.sum(jnp.where(ids == neg_row, 1.0, 0.0), axis=1, keepdims=True)
            picked = jnp.where(ids == tail_row, a, 0.0)
            positive = positive + (picked[0:8] + picked[8:16]) + (picked[16:24] + picked[24:32])
            score[rows] = (jnp.tanh(0.5 * a) + 1.0) * times * half
        positive = jnp.sum(positive, axis=0, keepdims=True)
        w_next = w_next + beside(3, 3)
        pos_grad = -jax.nn.sigmoid(-positive) * live
        for c in range(PART // 32):
            rows = slice(c * 32, (c + 1) * 32)
            ids = c * 32 + lax.broadcasted_iota(jnp.int32, (32, SPAN), 0)
            high, low = split(score[rows] + jnp.where(ids == tail_row, pos_grad, 0.0))
            c_high[rows] = high
            c_low[rows] = low
        both = mm(r_split[...], c_high[...])
        q_t = both[:D] + both[D:] + mm(r_split[0:D], c_low[...])
        high, low = split(q_t * w_now[...])
        cat[0:D] = high
        cat[D : 2 * D] = low
        z_t = jnp.concatenate(split(q_t * h_now[...]), axis=0)
        both = mm_nt(cat[...], hot[...])
        grad = both[:D] + both[D:]
        acc = ls_out[...] + jnp.mean(grad * grad, axis=0, keepdims=True)
        ls_out[...] = acc
        set_left(lt[...] - grad * (0.1 * lax.rsqrt(acc)))
        both = mm_nt(s3[0 : 2 * D], c_high[...])
        grad = both[:D] + both[D:] + mm_nt(s3[0:D], c_low[...])
        w_next = w_next + beside(6, 3)
        if second:
            z_last[...] = z_t
            w_next = x_ref[following]
        else:
            u_out[k] = z_t
        set_heads(following, w_next)
        acc = rs_out[...] + jnp.mean(grad * grad, axis=0, keepdims=True)
        rs_out[...] = acc
        set_right(rt[...] - grad * (0.1 * lax.rsqrt(acc)))
        return 0

    turns = block_turns(count_ref, turn)
    lax.fori_loop(0, turns, one, 0)
    l_out[...] = lt[...]
    if second:
        add_grads_part(row_of(rel_ref, turn, turns - 1), 0, 9, rel_hot, z_last[...], rel_acc)
        r_out[...] = rt[...]
        for c in range(REL // 256):
            side, column = (0, c) if c < CUT else (1, c - CUT)
            for half in range(2):
                rows = slice(c * 256 + half * 128, c * 256 + half * 128 + 128)
                g_out[2 * half + side][:, column * 256 : (column + 1) * 256] = rel_acc[rows]
    else:
        r_out[0:D, :] = rt[...]
        r_out[D : D + 8, :] = jnp.broadcast_to(rs_out[...], (8, PART))


def params():
    return pltpu.CompilerParams(vmem_limit_bytes=56 * 1024 * 1024)


def cost(flops):
    return pl.CostEstimate(flops=flops, bytes_accessed=8 * 2**20, transcendentals=0)


def flip_kernel(x_ref, y_ref, x_out, y_out):
    x_out[...] = x_ref[...].T
    y_out[...] = y_ref[...].T


def flip(x, y):
    return pl.pallas_call(
        flip_kernel,
        out_shape=[jax.ShapeDtypeStruct(x.shape[::-1], jnp.float32)] * 2,
        in_specs=[VMEM, VMEM],
        out_specs=[VMEM, VMEM],
        compiler_params=params(),
        cost_estimate=cost(0),
        name="flip",
    )(x, y)


def gather_rows(turn, count, rel, ops_split):
    return pl.pallas_call(
        lambda *refs: gather_kernel(turn, *refs),
        out_shape=jax.ShapeDtypeStruct((8, D, SPAN), jnp.float32),
        in_specs=[SMEM, VMEM, VMEM],
        out_specs=VMEM,
        compiler_params=params(),
        cost_estimate=cost(8 * 4 * REL * SPAN * D),
        name="gather_operators",
    )(count, rel, ops_split)


def relation_grads(turn, count, rel, z):
    return pl.pallas_call(
        lambda *refs: grads_kernel(turn, *refs),
        out_shape=jax.ShapeDtypeStruct((REL, D), jnp.float32),
        in_specs=[SMEM, VMEM, VMEM],
        out_specs=VMEM,
        compiler_params=params(),
        cost_estimate=cost(8 * 4 * REL * SPAN * D),
        name="relation_grads",
    )(count, rel, z)


def train(second, count, heads, tails, negs, rel, left, left_state, right, right_state, *others):
    f32, bf16 = jnp.float32, jnp.bfloat16
    sums = []
    if second:
        shapes = [((D, PART), f32), ((1, PART), f32), ((D, PART), f32), ((1, PART), f32)]
        shapes += [((128, CUT * D), f32), ((128, REL - CUT * D), f32)] * 2
        sums = [pltpu.VMEM((REL, D), f32), pltpu.VMEM((2 * D, SPAN), bf16)]
    else:
        shapes = [((D, PART), f32), ((1, PART), f32), ((D + 8, PART), f32), ((1, PART), f32)]
        shapes += [((8, 2 * D, SPAN), bf16), ((2 * D, REL), bf16)]
    return pl.pallas_call(
        lambda *refs: train_kernel(second, *refs),
        out_shape=[jax.ShapeDtypeStruct(*s) for s in shapes],
        in_specs=[SMEM] + [VMEM] * (8 + len(others)),
        out_specs=[VMEM] * len(shapes),
        scratch_shapes=[
            pltpu.VMEM((D, PART), f32),
            pltpu.VMEM((D, PART), f32),
            pltpu.VMEM((2 * D, PART), bf16),
            pltpu.VMEM((2 * D, PART), bf16),
            pltpu.VMEM((PART, 3 * D), bf16),
            pltpu.VMEM((PART, SPAN), bf16),
            pltpu.VMEM((3 * D, SPAN), bf16),
            pltpu.VMEM((2 * D, SPAN), bf16),
            pltpu.VMEM((PART, SPAN), f32),
            pltpu.VMEM((PART, SPAN), bf16),
            pltpu.VMEM((PART, SPAN), bf16),
            pltpu.VMEM((D, SPAN), f32),
            pltpu.VMEM((D, SPAN), f32),
            pltpu.VMEM((REL, SPAN), bf16),
        ]
        + sums,
        compiler_params=params(),
        name="train_second" if second else "train_first",
    )(count, heads, tails, negs, rel, left, left_state, right, right_state, *others)


def exchange(x, mask):
    return lax.ppermute(x, AXES, [(i, i ^ mask) for i in range(256)])


def trade(x, bits):
    groups = [[i | j for j in range(256) if j & ~bits == 0] for i in range(256) if i & bits == 0]
    return lax.all_to_all(x, AXES, 0, 0, tiled=True, axis_index_groups=groups)


def gather_over(x, masks):
    return jnp.concatenate([x] + [exchange(x, m) for m in masks], axis=0)


def sum_over(g, masks):
    n = g.shape[0] // (len(masks) + 1)
    total = g[:n]
    for j, m in enumerate(masks):
        total = total + exchange(g[(j + 1) * n : (j + 2) * n], m)
    return total


def gather_all(x):
    x = trade(jnp.broadcast_to(x.reshape(1, REL), (8, REL)), Z)
    first, last = x[:, : CUT * D], x[:, CUT * D :]
    first, last = gather_over(first, X), gather_over(last, Y)
    first, last = gather_over(first, Y), gather_over(last, X)
    return first, last, exchange(first, CORE), exchange(last, CORE)


def scatter_sum(first, last, first_sent, last_sent):
    first, last = first + exchange(first_sent, CORE), last + exchange(last_sent, CORE)
    first, last = sum_over(first, Y), sum_over(last, X)
    first, last = sum_over(first, X), sum_over(last, Y)
    return trade(jnp.concatenate([first, last], axis=1), Z).sum(axis=0).reshape(9, D)


def row_positions(relations):
    me = lax.axis_index(AXES)
    owner = relations * 7282 >> 16
    away = owner ^ me
    x = away >> 4 & 3
    y = away >> 3 & 1 | away >> 6 & 2
    piece = relations - owner * 9
    place = (owner & 7) | jnp.where(piece < CUT, x | y << 2, y | x << 2) << 3 | (away >> 6 & 1) << 7
    return piece * 256 + place


def move(mask, unit, right, beside, operands):
    def go(right, operands, m):
        moved = right
        if m:
            moved = lax.ppermute(right, "dom", [(i, i ^ m) for i in range(64)])
        return moved, beside(*operands)

    branches = [(lambda x, o, m=m: go(x, o, m)) for m in range(0, 8 * unit, unit)]
    return lax.switch(mask // unit & 7, branches, right, operands)


def body(left_table, left_state, right_table, right_state, operators, operator_state,
         heads, tails, relations, negatives, edge_counts, partner_mask):
    pieces = gather_all(operators)
    left_t, right_t = flip(left_table, right_table)
    rel = row_positions(relations)
    lists = (edge_counts, heads, tails, negatives, rel)
    left, ls, right, _, z, ops_split = train(
        False, *lists, left_t, left_state.reshape(1, PART), right_t, right_state.reshape(1, PART), *pieces
    )
    mask = partner_mask[0]
    right, w = move(mask, 1, right, lambda *x: gather_rows(1, *x), (edge_counts, rel, ops_split))
    right, g = move(mask, 8, right, lambda *x: relation_grads(0, *x), (edge_counts, rel, z))
    left, ls, right, rs, *sums = train(True, *lists, left, ls, right, ls, w, g)
    left, right = flip(left, right)
    grads = scatter_sum(*sums)
    new_acc = operator_state + grads * grads
    new_operators = operators - 0.5 * grads / jnp.sqrt(new_acc)
    return left, ls.reshape(PART), right, rs.reshape(PART), new_operators


def solution(mesh):
    whole = P(AXES)
    placed = (
        P(AXES, None), whole, P(AXES, None), whole, P(AXES, None), P(AXES, None),
        P(None, AXES), P(None, AXES), P(None, AXES), P(None, AXES, None), P(None, AXES), P(),
    )
    return jax.shard_map(
        body,
        mesh=mesh,
        in_specs=placed,
        out_specs=(P(AXES, None), whole, P(AXES, None), whole, P(AXES, None)),
        check_vma=False,
    )
```
